32 devices in a mesh: band: 4 (over y, x), slab: 8 (over z, core).
Axes of the slice: x: 2, y: 2, z: 4, core: 2. Of those that a mesh axis runs over, the one named last changes fastest.
Arguments:
- wavefunctions: float32 [4, 128, 128, 128], P('band', 'slab'), may hold values from -6 to 6
Outputs:
- exchange_field: float32 [4, 128, 128, 128], P('band', 'slab')
The draws below stay inside these ranges and needn't reach their ends.
All inputs are finite; a program needn't handle non-finite values.
Results may differ from the reference program's by a relative error of at most 0.0003.
Values sent between devices are 32-bit elements; how exact they have to be, the bound alone decides.
No kernel may reach another device: no remote copies, remote signals or barrier semaphores. Data moves between devices by JAX's collectives and lax.ppermute only.
A program may use at most 64 MiB of HBM per device.

```python
import jax
import jax.numpy as jnp
from jax import lax

GRID = 128
BANDS = 4


def block_levels(own_key, shape, pieces, low, largest):
    level, own = 1.0, jax.random.fold_in(own_key, 6)
    for position, parts in pieces:
        draws = jnp.exp(jax.random.uniform(jax.random.fold_in(own, position), (parts,), jnp.float32, low / len(pieces), largest / len(pieces)))
        level = level * jnp.repeat(draws, shape[position] // parts).reshape([-1 if axis == position else 1 for axis in range(len(shape))])
    return level


def normal_values(stream_key, shape, width, bound, pieces=(), held_as=jnp.bfloat16):
    entries = jax.random.normal(stream_key, shape, jnp.float32) * width
    if len(pieces) > 0:
        entries = block_levels(stream_key, shape, pieces, -0.22, 0.18) * entries
    return jnp.clip(entries, min=-bound, max=bound).astype(held_as)


def setup_inputs(seed: int = 0) -> dict:
    streams_of = jax.random.split(jax.random.key(seed), 2)
    return {
        "wavefunctions": normal_values(streams_of[0], (BANDS, GRID, GRID, GRID), 1.0, 6.0, ((0, 4), (1, 8)), jnp.float32),
    }


def coulomb_kernel(length):
    folded = jnp.fft.fftfreq(length) * length
    last_freq = jnp.arange(length // 2 + 1).astype(folded.dtype)
    squared = folded[:, None, None] ** 2 + folded[None, :, None] ** 2 + last_freq[None, None, :] ** 2
    kernel_scale = length ** 1.5 / 4.0
    return jnp.where(squared > 0, kernel_scale / jnp.maximum(squared, 1.0), 0.0)


def reference(wavefunctions):
    kernel = coulomb_kernel(GRID)

    def one_band(band_field):
        density = band_field[None] * wavefunctions
        spectra = jnp.fft.rfftn(density, axes=(1, 2, 3))
        potential = jnp.fft.irfftn(spectra * kernel, s=(GRID, GRID, GRID), axes=(1, 2, 3))
        return -0.25 * jnp.sum(potential * wavefunctions, axis=0)

    return lax.map(one_band, wavefunctions)
```

```python
import functools

import jax
import jax.numpy as jnp
import numpy as np
from jax import lax
from jax.experimental import pallas as pl
from jax.experimental.pallas import tpu as pltpu
from jax.sharding import PartitionSpec as P

HIGHEST_MODE = lax.Precision.HIGHEST
VMEM_LIMIT = 32 * 1024 * 1024


def cas_table(length):
    positions = np.arange(length)
    angles = 2.0 * np.pi / length * (positions[:, None] * positions[None, :] % length)
    return (np.cos(angles) + np.sin(angles)).astype(np.float32)


def squared_freqs(length):
    positions = np.arange(length)
    return (np.minimum(positions, length - positions) ** 2).astype(np.float32)


def coulomb(squared, length):
    kernel_scale = -0.25 * length**1.5 / 4.0 / float(length) ** 3
    return jnp.where(squared > 0, kernel_scale / jnp.maximum(squared, 1.0), 0.0)


def shifted(value, axis, steps):
    count = lax.axis_size(axis)
    pairs = [(source, (source + steps) % count) for source in range(count)]
    return lax.ppermute(value, axis, pairs)


def apply_table(form, field, table):
    return jnp.einsum(form, field, table, precision=HIGHEST_MODE)


def potentials(density):
    length = density.shape[2]
    table = jnp.asarray(cas_table(length))
    y_rows = length // lax.axis_size("slab")
    z_form = "pxyn,nk->pxyk"
    y_form = "pxnz,nk->pxkz"
    x_form = "pnyz,nk->pkyz"
    squared = jnp.asarray(squared_freqs(length))
    own_squared = lax.dynamic_slice_in_dim(squared, lax.axis_index("slab") * y_rows, y_rows)
    spec = apply_table(y_form, apply_table(z_form, density, table), table)
    spec = lax.all_to_all(spec, "slab", split_axis=2, concat_axis=1, tiled=True)
    spec = apply_table(x_form, spec, table) * coulomb(
        squared[:, None, None] + own_squared[None, :, None] + squared[None, None, :], length
    )
    spec = apply_table(x_form, spec, table)
    spec = lax.all_to_all(spec, "slab", split_axis=1, concat_axis=2, tiled=True)
    return apply_table(z_form, apply_table(y_form, spec, table), table)


def select_sum(selector, fields):
    return jnp.einsum("pb,pxyz->bxyz", selector, fields, precision=HIGHEST_MODE)


def general_device(wavefunctions):
    band_count = wavefunctions.shape[0]
    columns = lax.axis_size("band")
    half_loop = columns // 2
    left_index, right_index = np.triu_indices(band_count)
    left_select = (left_index[:, None] == np.arange(band_count)[None, :]).astype(np.float32)
    right_select = (
        (right_index[:, None] == np.arange(band_count)[None, :])
        & (left_index != right_index)[:, None]
    ).astype(np.float32)
    local_pots = potentials(wavefunctions[left_index] * wavefunctions[right_index])
    total_sum = select_sum(jnp.asarray(left_select), local_pots * wavefunctions[right_index])
    total_sum = total_sum + select_sum(
        jnp.asarray(right_select), local_pots * wavefunctions[left_index]
    )
    field_shape = wavefunctions.shape[1:]
    visitor = wavefunctions
    carried = jnp.zeros_like(wavefunctions)
    for shift_step in range(1, half_loop + 1):
        visitor, carried = shifted((visitor, carried), "band", 1)
        pair_density = (wavefunctions[:, None] * visitor[None, :]).reshape(
            (band_count * band_count,) + field_shape
        )
        pair_pots = potentials(pair_density).reshape((band_count, band_count) + field_shape)
        total_sum = total_sum + jnp.sum(pair_pots * visitor[None, :], axis=1)
        if shift_step < half_loop:
            contrib = jnp.sum(pair_pots * wavefunctions[:, None], axis=0)
        else:
            contrib = jnp.zeros_like(wavefunctions)
        carried = carried + contrib
    return total_sum + shifted(carried, "band", -half_loop)


def split_parts(value):
    high = value.astype(jnp.bfloat16)
    low = (value - high.astype(jnp.float32)).astype(jnp.bfloat16)
    return high, low


def product(left, right):
    return jnp.dot(left, right, preferred_element_type=jnp.float32)


def left_table(table):
    high, low = split_parts(table)
    if table.shape[1] <= 64:
        return jnp.concatenate([high, high, low], axis=1)
    return jnp.concatenate(
        [
            jnp.concatenate([high, high], axis=1),
            jnp.concatenate([low, jnp.zeros_like(low)], axis=1),
        ],
        axis=0,
    )


def left_apply(parts, value):
    high, low = split_parts(value)
    if value.shape[0] <= 64:
        return product(parts, jnp.concatenate([high, low, high], axis=0))
    both = product(parts, jnp.concatenate([high, low], axis=0))
    rows = parts.shape[0] // 2
    return both[:rows] + both[rows:]


def right_table(table):
    high, low = split_parts(table)
    return jnp.concatenate(
        [
            jnp.concatenate([high, low], axis=1),
            jnp.concatenate([high, jnp.zeros_like(low)], axis=1),
        ],
        axis=0,
    )


def right_apply(value, parts):
    both = product(jnp.concatenate(split_parts(value), axis=1), parts)
    columns = parts.shape[1] // 2
    return both[:, :columns] + both[:, columns:]


def two_planes(ref, first):
    return jnp.concatenate([ref[first], ref[first + 1]], axis=1)


def store_two(ref, first, value):
    length = ref.shape[2]
    ref[first] = value[:, :length]
    ref[first + 1] = value[:, length:]


def partner_masks(slabs):
    far = list(range(slabs - 1, slabs // 2 - 1, -1))
    near = list(range(1, slabs // 2)) + [0]
    return [mask for pair in zip(far, near) for mask in pair] if slabs > 1 else [0]


def own_masks(slabs):
    return [chip + core for chip in range(slabs - 2, -1, -2) for core in range(2)]


def masks_of(fields, slabs):
    return own_masks(slabs) if len(fields) == 1 else partner_masks(slabs)


def partner_rows(table_ref, masks, start, size):
    slab = lax.axis_index("slab")
    return jnp.concatenate(
        [
            table_ref[pl.ds(start + lax.bitwise_xor(slab, mask) * size, size), :]
            for mask in masks
        ],
        axis=0,
    )


def half_groups():
    column = lax.axis_index("band")
    return lax.rem(column, 2), lax.div(column, 2)


def group_starts(fields, length):
    if len(fields) == 1:
        return [0]
    return [group * (length // 2) for group in half_groups()]


def y_tables(fields, slabs, table_ref):
    starts = group_starts(fields, table_ref.shape[0])
    size = table_ref.shape[0] // slabs // (1 if len(fields) == 1 else 2)
    masks = masks_of(fields, slabs)
    return [partner_rows(table_ref, masks, start, size) for start in starts]


def forward_kernel(fields, slabs, bands, table_ref, *rest):
    psi_refs, out_refs, held = rest[:bands], rest[bands:-1], rest[-1]
    planes, length = psi_refs[0].shape[:2]
    per_slab = out_refs[0].shape[1]
    rows = held.shape[1] // planes
    y_parts = [left_table(table) for table in y_tables(fields, slabs, table_ref)]
    z_parts = right_table(table_ref[...])
    piece = per_slab * planes
    for first in range(0, planes, 2):
        psi = [two_planes(ref, first) for ref in psi_refs]
        for f, (a, b, group) in enumerate(fields):
            spec = left_apply(y_parts[group], psi[a] * psi[b])
            for side in range(2):
                held[f, pl.ds(first + side, rows, stride=planes), :] = spec[
                    :, side * length : (side + 1) * length
                ]
    for k, ref in enumerate(out_refs):
        for f in range(len(fields)):
            spec = right_apply(held[f, k * piece : (k + 1) * piece, :], z_parts)
            ref[f] = spec.reshape(per_slab, planes, length)


def folded_square(position, length):
    folded = jnp.minimum(position, length - position)
    return (folded * folded).astype(jnp.float32)


def middle_kernel(fields, slabs, table_ref, *rest):
    if len(fields) == 1:
        *chip_refs, swap_ref, kept_ref, swapped_ref = rest
        per_slab = chip_refs[0].shape[1] // 2
        in_refs, out_refs = [], []
        for n, ref in enumerate(chip_refs):
            half = pl.ds(n * per_slab, per_slab)
            in_refs += [ref.at[:, pl.ds(0, per_slab)], swap_ref.at[:, half]]
            out_refs += [kept_ref.at[:, half], swapped_ref.at[:, half]]
    else:
        in_refs, out_refs = rest[:slabs], rest[slabs:]
    _, per_slab, planes, length = in_refs[0].shape
    back_table = partner_rows(table_ref, masks_of(fields, slabs), 0, planes)
    x_parts, back_parts = left_table(back_table.T), left_table(back_table)
    in_plane = folded_square(
        lax.broadcasted_iota(jnp.int32, (length, length), 0), length
    ) + folded_square(lax.broadcasted_iota(jnp.int32, (length, length), 1), length)
    own_start = lax.axis_index("slab") * per_slab
    starts = [start + own_start for start in group_starts(fields, length)]
    for j in range(0, per_slab, 2):
        factors = [
            jnp.concatenate(
                [
                    coulomb(in_plane + folded_square(start + j + side, length), length)
                    for side in range(2)
                ],
                axis=1,
            )
            for start in starts
        ]
        for f, (_, _, group) in enumerate(fields):
            wide = jnp.concatenate(
                [
                    jnp.concatenate([ref[f, j + side] for ref in in_refs], axis=0)
                    for side in range(2)
                ],
                axis=1,
            )
            back = left_apply(back_parts, left_apply(x_parts, wide) * factors[group])
            for k, ref in enumerate(out_refs):
                for side in range(2):
                    ref[f, j + side] = back[
                        k * planes : (k + 1) * planes, side * length : (side + 1) * length
                    ]


def two_potentials(y_parts, held, f, first, planes):
    rows = held.shape[1] // planes
    spec = jnp.concatenate(
        [held[f, pl.ds(first + side, rows, stride=planes), :] for side in range(2)], axis=1
    )
    return left_apply(y_parts, spec)


def backward_kernel(fields, slabs, arrays, bands, table_ref, *rest):
    spec_refs, psi_refs = rest[:arrays], rest[arrays : arrays + bands]
    term_refs, out_refs, held = rest[arrays + bands : -bands - 1], rest[-bands - 1 : -1], rest[-1]
    _, per_slab, planes, length = spec_refs[0].shape
    z_parts = right_table(table_ref[...])
    y_parts = [left_table(table.T) for table in y_tables(fields, slabs, table_ref)]
    rows = per_slab * planes
    for k, ref in enumerate(spec_refs):
        for f in range(len(fields)):
            held[f, k * rows : (k + 1) * rows, :] = right_apply(
                ref[f].reshape(rows, length), z_parts
            )
    for first in range(0, planes, 2):
        psi = [two_planes(ref, first) for ref in psi_refs]
        sums = [None] * bands
        for ref in term_refs:
            term = two_planes(ref, first)
            sums[0] = term if sums[0] is None else sums[0] + term
        for f, (a, b, group) in enumerate(fields):
            pot = two_potentials(y_parts[group], held, f, first, planes)
            for i, j in ((a, b),) if a == b else ((a, b), (b, a)):
                term = pot * psi[j]
                sums[i] = term if sums[i] is None else sums[i] + term
        for ref, total in zip(out_refs, sums):
            store_two(ref, first, total)


def permuted(value, axis, mask):
    count = lax.axis_size(axis)
    return lax.ppermute(value, axis, [(source, source ^ mask) for source in range(count)])


def exchanged(blocks, masks):
    return [
        permuted(block, "slab", mask) if mask else block for block, mask in zip(blocks, masks)
    ]


def paired_device(wavefunctions):
    _, planes, length, _ = wavefunctions.shape
    slabs = lax.axis_size("slab")
    table = jnp.asarray(cas_table(length))

    def call(body, shape, count, held, *operands):
        return pl.pallas_call(
            body,
            out_shape=[jax.ShapeDtypeStruct(shape, jnp.float32)] * count,
            scratch_shapes=[pltpu.VMEM(held, jnp.float32)] if held else [],
            compiler_params=pltpu.CompilerParams(vmem_limit_bytes=VMEM_LIMIT),
        )(table, *operands)

    own_pair = [(0, 0, 0)]
    cross_pairs = [(0, 1, 0), (0, 2, 1), (1, 2, 1)]
    own_rows, cross_rows = length // slabs, length // 2 // slabs
    own_held = (1, length * planes, length)
    cross_held = (3, length // 2 * planes, length)
    own_chips, cross_masks = own_masks(slabs)[::2], partner_masks(slabs)
    own_block = (1, 2 * own_rows, planes, length)
    cross_block = (3, cross_rows, planes, length)
    swap_block = (1, length // 2, planes, length)

    def forward(fields, block, count, held, *bands):
        body = functools.partial(forward_kernel, fields, slabs, len(bands))
        return call(body, block, count, held, *bands)

    def middle(fields, block, count, *blocks):
        body = functools.partial(middle_kernel, fields, slabs)
        return call(body, block, count, None, *blocks)

    def backward(fields, blocks, bands, terms, held):
        body = functools.partial(backward_kernel, fields, slabs, len(blocks), len(bands))
        shape = (planes, length, length)
        return call(body, shape, len(bands), held, *blocks, *bands, *terms)

    psi = wavefunctions[0]
    bands = [psi, permuted(psi, "band", 1), permuted(psi, "band", 2)]
    chips = exchanged(forward(own_pair, own_block, len(own_chips), own_held, psi), own_chips)
    cross_spec = forward(cross_pairs, cross_block, slabs, cross_held, *bands)
    cross_spec = exchanged(cross_spec, cross_masks)
    chips, cross_spec[0] = lax.optimization_barrier((chips, cross_spec[0]))
    swap = jnp.concatenate([chip[:, own_rows:] for chip in chips], axis=1)
    kept, swap = middle(own_pair, swap_block, 2, *chips, permuted(swap, "slab", 1))
    swap = permuted(swap, "slab", 1)
    chips = [
        jnp.concatenate([part[:, n * own_rows : (n + 1) * own_rows] for part in (kept, swap)], axis=1)
        for n in range(len(own_chips))
    ]
    cross_spec = middle(cross_pairs, cross_block, slabs, *cross_spec)
    cross_spec = exchanged(cross_spec, cross_masks)
    chips, cross_spec = lax.optimization_barrier((chips, cross_spec))
    chips = exchanged(chips, own_chips)
    own_sum, to_x, to_y = backward(cross_pairs, cross_spec, bands, [], cross_held)
    sums = [own_sum, permuted(to_x, "band", 1), permuted(to_y, "band", 2)]
    (total,) = backward(own_pair, chips, [psi], sums, own_held)
    return total[None]


def per_device(wavefunctions):
    length = wavefunctions.shape[2]
    columns, slabs = lax.axis_size("band"), lax.axis_size("slab")
    fits = (
        wavefunctions.shape[0] == 1
        and columns == 4
        and length == 128
        and wavefunctions.shape[1] % 8 == 0
        and slabs & (slabs - 1) == 0
        and slabs > 1
        and length % (4 * slabs) == 0
    )
    return paired_device(wavefunctions) if fits else general_device(wavefunctions)


def solution(mesh):
    in_specs = (P("band", "slab", None, None),)
    out_specs = P("band", "slab", None, None)
    return jax.shard_map(
        per_device, mesh=mesh, in_specs=in_specs, out_specs=out_specs, check_vma=False
    )
```

```python
import functools

import jax
import jax.numpy as jnp
import numpy as np
from jax import lax
from jax.experimental import pallas as pl
from jax.experimental.pallas import tpu as pltpu
from jax.sharding import PartitionSpec as P

HIGHEST_MODE = lax.Precision.HIGHEST
VMEM_LIMIT = 32 * 1024 * 1024


def cas_table(length):
    positions = np.arange(length)
    angles = 2.0 * np.pi / length * (positions[:, None] * positions[None, :] % length)
    return (np.cos(angles) + np.sin(angles)).astype(np.float32)


def squared_freqs(length):
    positions = np.arange(length)
    return (np.minimum(positions, length - positions) ** 2).astype(np.float32)


def coulomb(squared, length):
    kernel_scale = -0.25 * length**1.5 / 4.0 / float(length) ** 3
    return jnp.where(squared > 0, kernel_scale / jnp.maximum(squared, 1.0), 0.0)


def shifted(value, axis, steps):
    count = lax.axis_size(axis)
    pairs = [(source, (source + steps) % count) for source in range(count)]
    return lax.ppermute(value, axis, pairs)


def apply_table(form, field, table):
    return jnp.einsum(form, field, table, precision=HIGHEST_MODE)


def potentials(density):
    length = density.shape[2]
    table = jnp.asarray(cas_table(length))
    y_rows = length // lax.axis_size("slab")
    z_form = "pxyn,nk->pxyk"
    y_form = "pxnz,nk->pxkz"
    x_form = "pnyz,nk->pkyz"
    squared = jnp.asarray(squared_freqs(length))
    own_squared = lax.dynamic_slice_in_dim(squared, lax.axis_index("slab") * y_rows, y_rows)
    spec = apply_table(y_form, apply_table(z_form, density, table), table)
    spec = lax.all_to_all(spec, "slab", split_axis=2, concat_axis=1, tiled=True)
    spec = apply_table(x_form, spec, table) * coulomb(
        squared[:, None, None] + own_squared[None, :, None] + squared[None, None, :], length
    )
    spec = apply_table(x_form, spec, table)
    spec = lax.all_to_all(spec, "slab", split_axis=1, concat_axis=2, tiled=True)
    return apply_table(z_form, apply_table(y_form, spec, table), table)


def select_sum(selector, fields):
    return jnp.einsum("pb,pxyz->bxyz", selector, fields, precision=HIGHEST_MODE)


def general_device(wavefunctions):
    band_count = wavefunctions.shape[0]
    columns = lax.axis_size("band")
    half_loop = columns // 2
    left_index, right_index = np.triu_indices(band_count)
    left_select = (left_index[:, None] == np.arange(band_count)[None, :]).astype(np.float32)
    right_select = (
        (right_index[:, None] == np.arange(band_count)[None, :])
        & (left_index != right_index)[:, None]
    ).astype(np.float32)
    local_pots = potentials(wavefunctions[left_index] * wavefunctions[right_index])
    total_sum = select_sum(jnp.asarray(left_select), local_pots * wavefunctions[right_index])
    total_sum = total_sum + select_sum(
        jnp.asarray(right_select), local_pots * wavefunctions[left_index]
    )
    field_shape = wavefunctions.shape[1:]
    visitor = wavefunctions
    carried = jnp.zeros_like(wavefunctions)
    for shift_step in range(1, half_loop + 1):
        visitor, carried = shifted((visitor, carried), "band", 1)
        pair_density = (wavefunctions[:, None] * visitor[None, :]).reshape(
            (band_count * band_count,) + field_shape
        )
        pair_pots = potentials(pair_density).reshape((band_count, band_count) + field_shape)
        total_sum = total_sum + jnp.sum(pair_pots * visitor[None, :], axis=1)
        if shift_step < half_loop:
            contrib = jnp.sum(pair_pots * wavefunctions[:, None], axis=0)
        else:
            contrib = jnp.zeros_like(wavefunctions)
        carried = carried + contrib
    return total_sum + shifted(carried, "band", -half_loop)


def split_parts(value):
    high = value.astype(jnp.bfloat16)
    low = (value - high.astype(jnp.float32)).astype(jnp.bfloat16)
    return high, low


def product(left, right):
    return jnp.dot(left, right, preferred_element_type=jnp.float32)


def left_table(table):
    high, low = split_parts(table)
    if table.shape[1] <= 64:
        return jnp.concatenate([high, high, low], axis=1)
    return jnp.concatenate(
        [
            jnp.concatenate([high, high], axis=1),
            jnp.concatenate([low, jnp.zeros_like(low)], axis=1),
        ],
        axis=0,
    )


def left_apply(parts, value):
    high, low = split_parts(value)
    if value.shape[0] <= 64:
        return product(parts, jnp.concatenate([high, low, high], axis=0))
    both = product(parts, jnp.concatenate([high, low], axis=0))
    rows = parts.shape[0] // 2
    return both[:rows] + both[rows:]


def right_table(table):
    high, low = split_parts(table)
    return jnp.concatenate(
        [
            jnp.concatenate([high, low], axis=1),
            jnp.concatenate([high, jnp.zeros_like(low)], axis=1),
        ],
        axis=0,
    )


def right_apply(value, parts):
    both = product(jnp.concatenate(split_parts(value), axis=1), parts)
    columns = parts.shape[1] // 2
    return both[:, :columns] + both[:, columns:]


def two_planes(ref, first):
    return jnp.concatenate([ref[first], ref[first + 1]], axis=1)


def store_two(ref, first, value):
    length = ref.shape[2]
    ref[first] = value[:, :length]
    ref[first + 1] = value[:, length:]


def partner_masks(slabs):
    far = list(range(slabs - 1, slabs // 2 - 1, -1))
    near = list(range(1, slabs // 2)) + [0]
    return [mask for pair in zip(far, near) for mask in pair] if slabs > 1 else [0]


def own_masks(slabs):
    return [chip + core for chip in range(slabs - 2, -1, -2) for core in range(2)]


def masks_of(fields, slabs):
    return own_masks(slabs) if len(fields) == 1 else partner_masks(slabs)


def partner_rows(table_ref, masks, start, size):
    slab = lax.axis_index("slab")
    return jnp.concatenate(
        [
            table_ref[pl.ds(start + lax.bitwise_xor(slab, mask) * size, size), :]
            for mask in masks
        ],
        axis=0,
    )


def half_groups():
    column = lax.axis_index("band")
    return lax.rem(column, 2), lax.div(column, 2)


def group_starts(fields, length):
    if len(fields) == 1:
        return [0]
    return [group * (length // 2) for group in half_groups()]


def y_tables(fields, slabs, table_ref):
    starts = group_starts(fields, table_ref.shape[0])
    size = table_ref.shape[0] // slabs // (1 if len(fields) == 1 else 2)
    masks = masks_of(fields, slabs)
    return [partner_rows(table_ref, masks, start, size) for start in starts]


def forward_kernel(fields, slabs, bands, table_ref, *rest):
    psi_refs, out_refs, held = rest[:bands], rest[bands:-1], rest[-1]
    planes, length = psi_refs[0].shape[:2]
    per_slab = out_refs[0].shape[1]
    rows = held.shape[1] // planes
    y_parts = [left_table(table) for table in y_tables(fields, slabs, table_ref)]
    z_parts = right_table(table_ref[...])
    piece = per_slab * planes
    for first in range(0, planes, 2):
        psi = [two_planes(ref, first) for ref in psi_refs]
        for f, (a, b, group) in enumerate(fields):
            spec = left_apply(y_parts[group], psi[a] * psi[b])
            for side in range(2):
                held[f, pl.ds(first + side, rows, stride=planes), :] = spec[
                    :, side * length : (side + 1) * length
                ]
    for k, ref in enumerate(out_refs):
        for f in range(len(fields)):
            spec = right_apply(held[f, k * piece : (k + 1) * piece, :], z_parts)
            ref[f] = spec.reshape(per_slab, planes, length)


def folded_square(position, length):
    folded = jnp.minimum(position, length - position)
    return (folded * folded).astype(jnp.float32)


def middle_kernel(fields, slabs, table_ref, *rest):
    if len(fields) == 1:
        *chip_refs, swap_ref, kept_ref, swapped_ref = rest
        per_slab = chip_refs[0].shape[1] // 2
        in_refs, out_refs = [], []
        for n, ref in enumerate(chip_refs):
            half = pl.ds(n * per_slab, per_slab)
            in_refs += [ref.at[:, pl.ds(0, per_slab)], swap_ref.at[:, half]]
            out_refs += [kept_ref.at[:, half], swapped_ref.at[:, half]]
    else:
        in_refs, out_refs = rest[:slabs], rest[slabs:]
    _, per_slab, planes, length = in_refs[0].shape
    back_table = partner_rows(table_ref, masks_of(fields, slabs), 0, planes)
    x_parts, back_parts = left_table(back_table.T), left_table(back_table)
    in_plane = folded_square(
        lax.broadcasted_iota(jnp.int32, (length, length), 0), length
    ) + folded_square(lax.broadcasted_iota(jnp.int32, (length, length), 1), length)
    own_start = lax.axis_index("slab") * per_slab
    starts = [start + own_start for start in group_starts(fields, length)]
    for j in range(0, per_slab, 2):
        factors = [
            jnp.concatenate(
                [
                    coulomb(in_plane + folded_square(start + j + side, length), length)
                    for side in range(2)
                ],
                axis=1,
            )
            for start in starts
        ]
        for f, (_, _, group) in enumerate(fields):
            wide = jnp.concatenate(
                [
                    jnp.concatenate([ref[f, j + side] for ref in in_refs], axis=0)
                    for side in range(2)
                ],
                axis=1,
            )
            back = left_apply(back_parts, left_apply(x_parts, wide) * factors[group])
            for k, ref in enumerate(out_refs):
                for side in range(2):
                    ref[f, j + side] = back[
                        k * planes : (k + 1) * planes, side * length : (side + 1) * length
                    ]


def two_potentials(y_parts, held, f, first, planes):
    rows = held.shape[1] // planes
    spec = jnp.concatenate(
        [held[f, pl.ds(first + side, rows, stride=planes), :] for side in range(2)], axis=1
    )
    return left_apply(y_parts, spec)


def backward_kernel(fields, slabs, arrays, bands, table_ref, *rest):
    spec_refs, psi_refs = rest[:arrays], rest[arrays : arrays + bands]
    term_refs, out_refs, held = rest[arrays + bands : -bands - 1], rest[-bands - 1 : -1], rest[-1]
    _, per_slab, planes, length = spec_refs[0].shape
    z_parts = right_table(table_ref[...])
    y_parts = [left_table(table.T) for table in y_tables(fields, slabs, table_ref)]
    rows = per_slab * planes
    for k, ref in enumerate(spec_refs):
        for f in range(len(fields)):
            held[f, k * rows : (k + 1) * rows, :] = right_apply(
                ref[f].reshape(rows, length), z_parts
            )
    for first in range(0, planes, 2):
        psi = [two_planes(ref, first) for ref in psi_refs]
        sums = [None] * bands
        for ref in term_refs:
            term = two_planes(ref, first)
            sums[0] = term if sums[0] is None else sums[0] + term
        for f, (a, b, group) in enumerate(fields):
            pot = two_potentials(y_parts[group], held, f, first, planes)
            for i, j in ((a, b),) if a == b else ((a, b), (b, a)):
                term = pot * psi[j]
                sums[i] = term if sums[i] is None else sums[i] + term
        for ref, total in zip(out_refs, sums):
            store_two(ref, first, total)


def permuted(value, axis, mask):
    count = lax.axis_size(axis)
    return lax.ppermute(value, axis, [(source, source ^ mask) for source in range(count)])


def exchanged(blocks, masks):
    return [
        permuted(block, "slab", mask) if mask else block for block, mask in zip(blocks, masks)
    ]


def paired_device(wavefunctions):
    _, planes, length, _ = wavefunctions.shape
    slabs = lax.axis_size("slab")
    table = jnp.asarray(cas_table(length))

    def call(body, shape, count, held, *operands):
        return pl.pallas_call(
            body,
            out_shape=[jax.ShapeDtypeStruct(shape, jnp.float32)] * count,
            scratch_shapes=[pltpu.VMEM(held, jnp.float32)] if held else [],
            compiler_params=pltpu.CompilerParams(vmem_limit_bytes=VMEM_LIMIT),
        )(table, *operands)

    own_pair = [(0, 0, 0)]
    cross_pairs = [(0, 1, 0), (0, 2, 1), (1, 2, 1)]
    own_rows, cross_rows = length // slabs, length // 2 // slabs
    own_held = (1, length * planes, length)
    cross_held = (3, length // 2 * planes, length)
    own_chips, cross_masks = own_masks(slabs)[::2], partner_masks(slabs)
    own_block = (1, 2 * own_rows, planes, length)
    cross_block = (3, cross_rows, planes, length)
    swap_block = (1, length // 2, planes, length)

    def forward(fields, block, count, held, *bands):
        body = functools.partial(forward_kernel, fields, slabs, len(bands))
        return call(body, block, count, held, *bands)

    def middle(fields, block, count, *blocks):
        body = functools.partial(middle_kernel, fields, slabs)
        return call(body, block, count, None, *blocks)

    def backward(fields, blocks, bands, terms, held):
        body = functools.partial(backward_kernel, fields, slabs, len(blocks), len(bands))
        shape = (planes, length, length)
        return call(body, shape, len(bands), held, *blocks, *bands, *terms)

    psi = wavefunctions[0]
    bands = [psi, permuted(psi, "band", 1), permuted(psi, "band", 2)]
    chips = exchanged(forward(own_pair, own_block, len(own_chips), own_held, psi), own_chips)
    cross_spec = forward(cross_pairs, cross_block, slabs, cross_held, *bands)
    cross_spec = exchanged(cross_spec, cross_masks)
    late = slabs // 2
    chips, cross_spec[late] = lax.optimization_barrier((chips, cross_spec[late]))
    swap = jnp.concatenate([chip[:, own_rows:] for chip in chips], axis=1)
    kept, swap = middle(own_pair, swap_block, 2, *chips, permuted(swap, "slab", 1))
    swap = permuted(swap, "slab", 1)
    chips = [
        jnp.concatenate([part[:, n * own_rows : (n + 1) * own_rows] for part in (kept, swap)], axis=1)
        for n in range(len(own_chips))
    ]
    cross_spec = middle(cross_pairs, cross_block, slabs, *cross_spec)
    cross_spec = exchanged(cross_spec, cross_masks)
    chips, cross_spec = lax.optimization_barrier((chips, cross_spec))
    chips = exchanged(chips, own_chips)
    own_sum, to_x, to_y = backward(cross_pairs, cross_spec, bands, [], cross_held)
    sums = [own_sum, permuted(to_x, "band", 1), permuted(to_y, "band", 2)]
    (total,) = backward(own_pair, chips, [psi], sums, own_held)
    return total[None]


def per_device(wavefunctions):
    length = wavefunctions.shape[2]
    columns, slabs = lax.axis_size("band"), lax.axis_size("slab")
    fits = (
        wavefunctions.shape[0] == 1
        and columns == 4
        and length == 128
        and wavefunctions.shape[1] % 8 == 0
        and slabs & (slabs - 1) == 0
        and slabs > 1
        and length % (4 * slabs) == 0
    )
    return paired_device(wavefunctions) if fits else general_device(wavefunctions)


def solution(mesh):
    in_specs = (P("band", "slab", None, None),)
    out_specs = P("band", "slab", None, None)
    return jax.shard_map(
        per_device, mesh=mesh, in_specs=in_specs, out_specs=out_specs, check_vma=False
    )
```

```python
import functools

import jax
import jax.numpy as jnp
import numpy as np
from jax import lax
from jax.experimental import pallas as pl
from jax.experimental.pallas import tpu as pltpu
from jax.sharding import PartitionSpec as P

HIGHEST_MODE = lax.Precision.HIGHEST
VMEM_LIMIT = 32 * 1024 * 1024


def cas_table(length):
    positions = np.arange(length)
    angles = 2.0 * np.pi / length * (positions[:, None] * positions[None, :] % length)
    return (np.cos(angles) + np.sin(angles)).astype(np.float32)


def squared_freqs(length):
    positions = np.arange(length)
    return (np.minimum(positions, length - positions) ** 2).astype(np.float32)


def coulomb(squared, length):
    kernel_scale = -0.25 * length**1.5 / 4.0 / float(length) ** 3
    return jnp.where(squared > 0, kernel_scale / jnp.maximum(squared, 1.0), 0.0)


def shifted(value, axis, steps):
    count = lax.axis_size(axis)
    pairs = [(source, (source + steps) % count) for source in range(count)]
    return lax.ppermute(value, axis, pairs)


def apply_table(form, field, table):
    return jnp.einsum(form, field, table, precision=HIGHEST_MODE)


def potentials(density):
    length = density.shape[2]
    table = jnp.asarray(cas_table(length))
    y_rows = length // lax.axis_size("slab")
    z_form = "pxyn,nk->pxyk"
    y_form = "pxnz,nk->pxkz"
    x_form = "pnyz,nk->pkyz"
    squared = jnp.asarray(squared_freqs(length))
    own_squared = lax.dynamic_slice_in_dim(squared, lax.axis_index("slab") * y_rows, y_rows)
    spec = apply_table(y_form, apply_table(z_form, density, table), table)
    spec = lax.all_to_all(spec, "slab", split_axis=2, concat_axis=1, tiled=True)
    spec = apply_table(x_form, spec, table) * coulomb(
        squared[:, None, None] + own_squared[None, :, None] + squared[None, None, :], length
    )
    spec = apply_table(x_form, spec, table)
    spec = lax.all_to_all(spec, "slab", split_axis=1, concat_axis=2, tiled=True)
    return apply_table(z_form, apply_table(y_form, spec, table), table)


def select_sum(selector, fields):
    return jnp.einsum("pb,pxyz->bxyz", selector, fields, precision=HIGHEST_MODE)


def general_device(wavefunctions):
    band_count = wavefunctions.shape[0]
    columns = lax.axis_size("band")
    half_loop = columns // 2
    left_index, right_index = np.triu_indices(band_count)
    left_select = (left_index[:, None] == np.arange(band_count)[None, :]).astype(np.float32)
    right_select = (
        (right_index[:, None] == np.arange(band_count)[None, :])
        & (left_index != right_index)[:, None]
    ).astype(np.float32)
    local_pots = potentials(wavefunctions[left_index] * wavefunctions[right_index])
    total_sum = select_sum(jnp.asarray(left_select), local_pots * wavefunctions[right_index])
    total_sum = total_sum + select_sum(
        jnp.asarray(right_select), local_pots * wavefunctions[left_index]
    )
    field_shape = wavefunctions.shape[1:]
    visitor = wavefunctions
    carried = jnp.zeros_like(wavefunctions)
    for shift_step in range(1, half_loop + 1):
        visitor, carried = shifted((visitor, carried), "band", 1)
        pair_density = (wavefunctions[:, None] * visitor[None, :]).reshape(
            (band_count * band_count,) + field_shape
        )
        pair_pots = potentials(pair_density).reshape((band_count, band_count) + field_shape)
        total_sum = total_sum + jnp.sum(pair_pots * visitor[None, :], axis=1)
        if shift_step < half_loop:
            contrib = jnp.sum(pair_pots * wavefunctions[:, None], axis=0)
        else:
            contrib = jnp.zeros_like(wavefunctions)
        carried = carried + contrib
    return total_sum + shifted(carried, "band", -half_loop)


def split_parts(value):
    high = value.astype(jnp.bfloat16)
    low = (value - high.astype(jnp.float32)).astype(jnp.bfloat16)
    return high, low


def product(left, right):
    return jnp.dot(left, right, preferred_element_type=jnp.float32)


def left_table(table):
    high, low = split_parts(table)
    if table.shape[1] <= 64:
        return jnp.concatenate([high, high, low], axis=1)
    return jnp.concatenate(
        [
            jnp.concatenate([high, high], axis=1),
            jnp.concatenate([low, jnp.zeros_like(low)], axis=1),
        ],
        axis=0,
    )


def left_apply(parts, value):
    high, low = split_parts(value)
    if value.shape[0] <= 64:
        return product(parts, jnp.concatenate([high, low, high], axis=0))
    both = product(parts, jnp.concatenate([high, low], axis=0))
    rows = parts.shape[0] // 2
    return both[:rows] + both[rows:]


def right_table(table):
    high, low = split_parts(table)
    return jnp.concatenate(
        [
            jnp.concatenate([high, low], axis=1),
            jnp.concatenate([high, jnp.zeros_like(low)], axis=1),
        ],
        axis=0,
    )


def right_apply(value, parts):
    both = product(jnp.concatenate(split_parts(value), axis=1), parts)
    columns = parts.shape[1] // 2
    return both[:, :columns] + both[:, columns:]


def two_planes(ref, first):
    return jnp.concatenate([ref[first], ref[first + 1]], axis=1)


def store_two(ref, first, value):
    length = ref.shape[2]
    ref[first] = value[:, :length]
    ref[first + 1] = value[:, length:]


def partner_masks(slabs):
    far = list(range(slabs - 1, slabs // 2 - 1, -1))
    near = list(range(1, slabs // 2)) + [0]
    return [mask for pair in zip(far, near) for mask in pair] if slabs > 1 else [0]


def back_masks(slabs):
    masks = partner_masks(slabs)
    for n in range(0, slabs - 2, 2):
        masks[n], masks[n + 1] = masks[n + 1], masks[n]
    return masks


def own_masks(slabs):
    return [chip + core for chip in range(slabs - 2, -1, -2) for core in range(2)]


def masks_of(fields, slabs, back=False):
    if len(fields) == 1:
        return own_masks(slabs)
    return back_masks(slabs) if back else partner_masks(slabs)


def partner_rows(table_ref, masks, start, size):
    slab = lax.axis_index("slab")
    return jnp.concatenate(
        [
            table_ref[pl.ds(start + lax.bitwise_xor(slab, mask) * size, size), :]
            for mask in masks
        ],
        axis=0,
    )


def half_groups():
    column = lax.axis_index("band")
    return lax.rem(column, 2), lax.div(column, 2)


def group_starts(fields, length):
    if len(fields) == 1:
        return [0]
    return [group * (length // 2) for group in half_groups()]


def y_tables(fields, slabs, table_ref, back=False):
    starts = group_starts(fields, table_ref.shape[0])
    size = table_ref.shape[0] // slabs // (1 if len(fields) == 1 else 2)
    masks = masks_of(fields, slabs, back)
    return [partner_rows(table_ref, masks, start, size) for start in starts]


def forward_kernel(fields, slabs, bands, table_ref, *rest):
    psi_refs, out_refs, held = rest[:bands], rest[bands:-1], rest[-1]
    planes, length = psi_refs[0].shape[:2]
    per_slab = out_refs[0].shape[1]
    rows = held.shape[1] // planes
    y_parts = [left_table(table) for table in y_tables(fields, slabs, table_ref)]
    z_parts = right_table(table_ref[...])
    piece = per_slab * planes
    for first in range(0, planes, 2):
        psi = [two_planes(ref, first) for ref in psi_refs]
        for f, (a, b, group) in enumerate(fields):
            spec = left_apply(y_parts[group], psi[a] * psi[b])
            for side in range(2):
                held[f, pl.ds(first + side, rows, stride=planes), :] = spec[
                    :, side * length : (side + 1) * length
                ]
    for k, ref in enumerate(out_refs):
        for f in range(len(fields)):
            spec = right_apply(held[f, k * piece : (k + 1) * piece, :], z_parts)
            ref[f] = spec.reshape(per_slab, planes, length)


def folded_square(position, length):
    folded = jnp.minimum(position, length - position)
    return (folded * folded).astype(jnp.float32)


def middle_kernel(fields, slabs, table_ref, *rest):
    if len(fields) == 1:
        *chip_refs, swap_ref, kept_ref, swapped_ref = rest
        per_slab = chip_refs[0].shape[1] // 2
        in_refs, out_refs = [], []
        for n, ref in enumerate(chip_refs):
            half = pl.ds(n * per_slab, per_slab)
            in_refs += [ref.at[:, pl.ds(0, per_slab)], swap_ref.at[:, half]]
            out_refs += [kept_ref.at[:, half], swapped_ref.at[:, half]]
    else:
        in_refs, out_refs = rest[:slabs], rest[slabs:]
    _, per_slab, planes, length = in_refs[0].shape
    x_table, back_table = (
        partner_rows(table_ref, masks_of(fields, slabs, back), 0, planes)
        for back in (False, True)
    )
    x_parts, back_parts = left_table(x_table.T), left_table(back_table)
    in_plane = folded_square(
        lax.broadcasted_iota(jnp.int32, (length, length), 0), length
    ) + folded_square(lax.broadcasted_iota(jnp.int32, (length, length), 1), length)
    own_start = lax.axis_index("slab") * per_slab
    starts = [start + own_start for start in group_starts(fields, length)]
    for j in range(0, per_slab, 2):
        factors = [
            jnp.concatenate(
                [
                    coulomb(in_plane + folded_square(start + j + side, length), length)
                    for side in range(2)
                ],
                axis=1,
            )
            for start in starts
        ]
        for f, (_, _, group) in enumerate(fields):
            wide = jnp.concatenate(
                [
                    jnp.concatenate([ref[f, j + side] for ref in in_refs], axis=0)
                    for side in range(2)
                ],
                axis=1,
            )
            back = left_apply(back_parts, left_apply(x_parts, wide) * factors[group])
            for k, ref in enumerate(out_refs):
                for side in range(2):
                    ref[f, j + side] = back[
                        k * planes : (k + 1) * planes, side * length : (side + 1) * length
                    ]


def two_potentials(y_parts, held, f, first, planes):
    rows = held.shape[1] // planes
    spec = jnp.concatenate(
        [held[f, pl.ds(first + side, rows, stride=planes), :] for side in range(2)], axis=1
    )
    return left_apply(y_parts, spec)


def backward_kernel(fields, slabs, arrays, bands, table_ref, *rest):
    spec_refs, psi_refs = rest[:arrays], rest[arrays : arrays + bands]
    term_refs, out_refs, held = rest[arrays + bands : -bands - 1], rest[-bands - 1 : -1], rest[-1]
    _, per_slab, planes, length = spec_refs[0].shape
    z_parts = right_table(table_ref[...])
    y_parts = [left_table(table.T) for table in y_tables(fields, slabs, table_ref, True)]
    rows = per_slab * planes
    for k, ref in enumerate(spec_refs):
        for f in range(len(fields)):
            held[f, k * rows : (k + 1) * rows, :] = right_apply(
                ref[f].reshape(rows, length), z_parts
            )
    for first in range(0, planes, 2):
        psi = [two_planes(ref, first) for ref in psi_refs]
        sums = [None] * bands
        for ref in term_refs:
            term = two_planes(ref, first)
            sums[0] = term if sums[0] is None else sums[0] + term
        for f, (a, b, group) in enumerate(fields):
            pot = two_potentials(y_parts[group], held, f, first, planes)
            for i, j in ((a, b),) if a == b else ((a, b), (b, a)):
                term = pot * psi[j]
                sums[i] = term if sums[i] is None else sums[i] + term
        for ref, total in zip(out_refs, sums):
            store_two(ref, first, total)


def sum_kernel(_, first_ref, second_ref, third_ref, out_ref):
    out_ref[...] = first_ref[...] + second_ref[...] + third_ref[...]


def permuted(value, axis, mask):
    count = lax.axis_size(axis)
    return lax.ppermute(value, axis, [(source, source ^ mask) for source in range(count)])


def exchanged(blocks, masks):
    return [
        permuted(block, "slab", mask) if mask else block for block, mask in zip(blocks, masks)
    ]


def paired_device(wavefunctions):
    _, planes, length, _ = wavefunctions.shape
    slabs = lax.axis_size("slab")
    table = jnp.asarray(cas_table(length))

    def call(body, shape, count, held, *operands):
        return pl.pallas_call(
            body,
            out_shape=[jax.ShapeDtypeStruct(shape, jnp.float32)] * count,
            scratch_shapes=[pltpu.VMEM(held, jnp.float32)] if held else [],
            compiler_params=pltpu.CompilerParams(vmem_limit_bytes=VMEM_LIMIT),
        )(table, *operands)

    own_pair = [(0, 0, 0)]
    cross_pairs = [(0, 1, 0), (0, 2, 1), (1, 2, 1)]
    own_rows, cross_rows = length // slabs, length // 2 // slabs
    own_held = (1, length * planes, length)
    cross_held = (3, length // 2 * planes, length)
    own_chips, cross_masks = own_masks(slabs)[::2], partner_masks(slabs)
    own_block = (1, 2 * own_rows, planes, length)
    cross_block = (3, cross_rows, planes, length)
    swap_block = (1, length // 2, planes, length)

    def forward(fields, block, count, held, *bands):
        body = functools.partial(forward_kernel, fields, slabs, len(bands))
        return call(body, block, count, held, *bands)

    def middle(fields, block, count, *blocks):
        body = functools.partial(middle_kernel, fields, slabs)
        return call(body, block, count, None, *blocks)

    def backward(fields, blocks, bands, terms, held):
        body = functools.partial(backward_kernel, fields, slabs, len(blocks), len(bands))
        shape = (planes, length, length)
        return call(body, shape, len(bands), held, *blocks, *bands, *terms)

    psi = wavefunctions[0]
    bands = [psi, permuted(psi, "band", 1), permuted(psi, "band", 2)]
    chips = exchanged(forward(own_pair, own_block, len(own_chips), own_held, psi), own_chips)
    cross_spec = forward(cross_pairs, cross_block, slabs, cross_held, *bands)
    cross_spec = exchanged(cross_spec, cross_masks)
    chips, cross_spec[0] = lax.optimization_barrier((chips, cross_spec[0]))
    swap = jnp.concatenate([chip[:, own_rows:] for chip in chips], axis=1)
    kept, swap = middle(own_pair, swap_block, 2, *chips, permuted(swap, "slab", 1))
    swap = permuted(swap, "slab", 1)
    chips = [
        jnp.concatenate([part[:, n * own_rows : (n + 1) * own_rows] for part in (kept, swap)], axis=1)
        for n in range(len(own_chips))
    ]
    cross_spec = middle(cross_pairs, cross_block, slabs, *cross_spec)
    cross_spec = exchanged(cross_spec, back_masks(slabs))
    chips, cross_spec = lax.optimization_barrier((chips, cross_spec))
    chips = exchanged(chips, own_chips)
    own_sum, to_x, to_y = backward(cross_pairs, cross_spec, bands, [], cross_held)
    (total,) = backward(own_pair, chips, [psi], [own_sum], own_held)
    sums = [total, permuted(to_x, "band", 1), permuted(to_y, "band", 2)]
    (total,) = call(sum_kernel, psi.shape, 1, None, *sums)
    return total[None]


def per_device(wavefunctions):
    length = wavefunctions.shape[2]
    columns, slabs = lax.axis_size("band"), lax.axis_size("slab")
    fits = (
        wavefunctions.shape[0] == 1
        and columns == 4
        and length == 128
        and wavefunctions.shape[1] % 8 == 0
        and slabs & (slabs - 1) == 0
        and slabs > 1
        and length % (4 * slabs) == 0
    )
    return paired_device(wavefunctions) if fits else general_device(wavefunctions)


def solution(mesh):
    in_specs = (P("band", "slab", None, None),)
    out_specs = P("band", "slab", None, None)
    return jax.shard_map(
        per_device, mesh=mesh, in_specs=in_specs, out_specs=out_specs, check_vma=False
    )
```

```python
import functools

import jax
import jax.numpy as jnp
import numpy as np
from jax import lax
from jax.experimental import pallas as pl
from jax.experimental.pallas import tpu as pltpu
from jax.sharding import PartitionSpec as P

HIGHEST_MODE = lax.Precision.HIGHEST
VMEM_LIMIT = 32 * 1024 * 1024


def cas_table(length):
    positions = np.arange(length)
    angles = 2.0 * np.pi / length * (positions[:, None] * positions[None, :] % length)
    return (np.cos(angles) + np.sin(angles)).astype(np.float32)


def squared_freqs(length):
    positions = np.arange(length)
    return (np.minimum(positions, length - positions) ** 2).astype(np.float32)


def coulomb(squared, length):
    kernel_scale = -0.25 * length**1.5 / 4.0 / float(length) ** 3
    return jnp.where(squared > 0, kernel_scale / jnp.maximum(squared, 1.0), 0.0)


def shifted(value, axis, steps):
    count = lax.axis_size(axis)
    pairs = [(source, (source + steps) % count) for source in range(count)]
    return lax.ppermute(value, axis, pairs)


def apply_table(form, field, table):
    return jnp.einsum(form, field, table, precision=HIGHEST_MODE)


def potentials(density):
    length = density.shape[2]
    table = jnp.asarray(cas_table(length))
    y_rows = length // lax.axis_size("slab")
    z_form = "pxyn,nk->pxyk"
    y_form = "pxnz,nk->pxkz"
    x_form = "pnyz,nk->pkyz"
    squared = jnp.asarray(squared_freqs(length))
    own_squared = lax.dynamic_slice_in_dim(squared, lax.axis_index("slab") * y_rows, y_rows)
    spec = apply_table(y_form, apply_table(z_form, density, table), table)
    spec = lax.all_to_all(spec, "slab", split_axis=2, concat_axis=1, tiled=True)
    spec = apply_table(x_form, spec, table) * coulomb(
        squared[:, None, None] + own_squared[None, :, None] + squared[None, None, :], length
    )
    spec = apply_table(x_form, spec, table)
    spec = lax.all_to_all(spec, "slab", split_axis=1, concat_axis=2, tiled=True)
    return apply_table(z_form, apply_table(y_form, spec, table), table)


def select_sum(selector, fields):
    return jnp.einsum("pb,pxyz->bxyz", selector, fields, precision=HIGHEST_MODE)


def general_device(wavefunctions):
    band_count = wavefunctions.shape[0]
    columns = lax.axis_size("band")
    half_loop = columns // 2
    left_index, right_index = np.triu_indices(band_count)
    left_select = (left_index[:, None] == np.arange(band_count)[None, :]).astype(np.float32)
    right_select = (
        (right_index[:, None] == np.arange(band_count)[None, :])
        & (left_index != right_index)[:, None]
    ).astype(np.float32)
    local_pots = potentials(wavefunctions[left_index] * wavefunctions[right_index])
    total_sum = select_sum(jnp.asarray(left_select), local_pots * wavefunctions[right_index])
    total_sum = total_sum + select_sum(
        jnp.asarray(right_select), local_pots * wavefunctions[left_index]
    )
    field_shape = wavefunctions.shape[1:]
    visitor = wavefunctions
    carried = jnp.zeros_like(wavefunctions)
    for shift_step in range(1, half_loop + 1):
        visitor, carried = shifted((visitor, carried), "band", 1)
        pair_density = (wavefunctions[:, None] * visitor[None, :]).reshape(
            (band_count * band_count,) + field_shape
        )
        pair_pots = potentials(pair_density).reshape((band_count, band_count) + field_shape)
        total_sum = total_sum + jnp.sum(pair_pots * visitor[None, :], axis=1)
        if shift_step < half_loop:
            contrib = jnp.sum(pair_pots * wavefunctions[:, None], axis=0)
        else:
            contrib = jnp.zeros_like(wavefunctions)
        carried = carried + contrib
    return total_sum + shifted(carried, "band", -half_loop)


def split_parts(value):
    high = value.astype(jnp.bfloat16)
    low = (value - high.astype(jnp.float32)).astype(jnp.bfloat16)
    return high, low


def product(left, right):
    return jnp.dot(left, right, preferred_element_type=jnp.float32)


def left_table(table):
    high, low = split_parts(table)
    if table.shape[1] <= 64:
        return jnp.concatenate([high, high, low], axis=1)
    return jnp.concatenate(
        [
            jnp.concatenate([high, high], axis=1),
            jnp.concatenate([low, jnp.zeros_like(low)], axis=1),
        ],
        axis=0,
    )


def left_apply(parts, value):
    high, low = split_parts(value)
    if value.shape[0] <= 64:
        return product(parts, jnp.concatenate([high, low, high], axis=0))
    both = product(parts, jnp.concatenate([high, low], axis=0))
    rows = parts.shape[0] // 2
    return both[:rows] + both[rows:]


def right_table(table):
    high, low = split_parts(table)
    return jnp.concatenate(
        [
            jnp.concatenate([high, low], axis=1),
            jnp.concatenate([high, jnp.zeros_like(low)], axis=1),
        ],
        axis=0,
    )


def right_apply(value, parts):
    both = product(jnp.concatenate(split_parts(value), axis=1), parts)
    columns = parts.shape[1] // 2
    return both[:, :columns] + both[:, columns:]


def two_planes(ref, first):
    return jnp.concatenate([ref[first], ref[first + 1]], axis=1)


def store_two(ref, first, value):
    length = ref.shape[2]
    ref[first] = value[:, :length]
    ref[first + 1] = value[:, length:]


def partner_masks(slabs):
    far = list(range(slabs - 1, slabs // 2 - 1, -1))
    near = list(range(1, slabs // 2)) + [0]
    return [mask for pair in zip(far, near) for mask in pair] if slabs > 1 else [0]


def back_masks(slabs):
    masks = partner_masks(slabs)
    for n in range(0, slabs - 2, 2):
        masks[n], masks[n + 1] = masks[n + 1], masks[n]
    return masks


def own_masks(slabs):
    return [chip + core for chip in range(slabs - 2, -1, -2) for core in range(2)]


def masks_of(fields, slabs, back=False):
    if len(fields) == 1:
        return own_masks(slabs)
    return back_masks(slabs) if back else partner_masks(slabs)


def partner_rows(table_ref, masks, start, size):
    slab = lax.axis_index("slab")
    return jnp.concatenate(
        [
            table_ref[pl.ds(start + lax.bitwise_xor(slab, mask) * size, size), :]
            for mask in masks
        ],
        axis=0,
    )


def half_groups():
    column = lax.axis_index("band")
    return lax.rem(column, 2), lax.div(column, 2)


def group_starts(fields, length):
    if len(fields) == 1:
        return [0]
    return [group * (length // 2) for group in half_groups()]


def y_tables(fields, slabs, table_ref, back=False):
    starts = group_starts(fields, table_ref.shape[0])
    size = table_ref.shape[0] // slabs // (1 if len(fields) == 1 else 2)
    masks = masks_of(fields, slabs, back)
    return [partner_rows(table_ref, masks, start, size) for start in starts]


def forward_kernel(fields, slabs, bands, table_ref, *rest):
    psi_refs, out_refs, held = rest[:bands], rest[bands:-1], rest[-1]
    planes, length = psi_refs[0].shape[:2]
    per_slab = out_refs[0].shape[1]
    rows = held.shape[1] // planes
    y_parts = [left_table(table) for table in y_tables(fields, slabs, table_ref)]
    z_parts = right_table(table_ref[...])
    piece = per_slab * planes
    for first in range(0, planes, 2):
        psi = [two_planes(ref, first) for ref in psi_refs]
        for f, (a, b, group) in enumerate(fields):
            spec = left_apply(y_parts[group], psi[a] * psi[b])
            for side in range(2):
                held[f, pl.ds(first + side, rows, stride=planes), :] = spec[
                    :, side * length : (side + 1) * length
                ]
    for k, ref in enumerate(out_refs):
        rows = [held[f, k * piece : (k + 1) * piece, :] for f in range(len(fields))]
        spec = right_apply(jnp.concatenate(rows, axis=0), z_parts)
        ref[...] = spec.reshape(ref.shape)


def folded_square(position, length):
    folded = jnp.minimum(position, length - position)
    return (folded * folded).astype(jnp.float32)


def middle_kernel(fields, slabs, table_ref, *rest):
    if len(fields) == 1:
        *chip_refs, swap_ref, kept_ref, swapped_ref = rest
        per_slab = chip_refs[0].shape[1] // 2
        in_refs, out_refs = [], []
        for n, ref in enumerate(chip_refs):
            half = pl.ds(n * per_slab, per_slab)
            in_refs += [ref.at[:, pl.ds(0, per_slab)], swap_ref.at[:, half]]
            out_refs += [kept_ref.at[:, half], swapped_ref.at[:, half]]
    else:
        in_refs, out_refs = rest[:slabs], rest[slabs:]
    _, per_slab, planes, length = in_refs[0].shape
    x_table, back_table = (
        partner_rows(table_ref, masks_of(fields, slabs, back), 0, planes)
        for back in (False, True)
    )
    x_parts, back_parts = left_table(x_table.T), left_table(back_table)
    in_plane = folded_square(
        lax.broadcasted_iota(jnp.int32, (length, length), 0), length
    ) + folded_square(lax.broadcasted_iota(jnp.int32, (length, length), 1), length)
    own_start = lax.axis_index("slab") * per_slab
    starts = [start + own_start for start in group_starts(fields, length)]
    for j in range(0, per_slab, 2):
        factors = [
            jnp.concatenate(
                [
                    coulomb(in_plane + folded_square(start + j + side, length), length)
                    for side in range(2)
                ],
                axis=1,
            )
            for start in starts
        ]
        for f, (_, _, group) in enumerate(fields):
            wide = jnp.concatenate(
                [
                    jnp.concatenate([ref[f, j + side] for ref in in_refs], axis=0)
                    for side in range(2)
                ],
                axis=1,
            )
            back = left_apply(back_parts, left_apply(x_parts, wide) * factors[group])
            for k, ref in enumerate(out_refs):
                for side in range(2):
                    ref[f, j + side] = back[
                        k * planes : (k + 1) * planes, side * length : (side + 1) * length
                    ]


def two_potentials(y_parts, held, f, first, planes):
    rows = held.shape[1] // planes
    spec = jnp.concatenate(
        [held[f, pl.ds(first + side, rows, stride=planes), :] for side in range(2)], axis=1
    )
    return left_apply(y_parts, spec)


def backward_kernel(fields, slabs, arrays, bands, table_ref, *rest):
    spec_refs, psi_refs = rest[:arrays], rest[arrays : arrays + bands]
    term_refs, out_refs, held = rest[arrays + bands : -bands - 1], rest[-bands - 1 : -1], rest[-1]
    _, per_slab, planes, length = spec_refs[0].shape
    z_parts = right_table(table_ref[...])
    y_parts = [left_table(table.T) for table in y_tables(fields, slabs, table_ref, True)]
    rows = per_slab * planes
    for k, ref in enumerate(spec_refs):
        spec = right_apply(ref[...].reshape(len(fields) * rows, length), z_parts)
        for f in range(len(fields)):
            held[f, k * rows : (k + 1) * rows, :] = spec[f * rows : (f + 1) * rows]
    for first in range(0, planes, 2):
        psi = [two_planes(ref, first) for ref in psi_refs]
        sums = [None] * bands
        for ref in term_refs:
            term = two_planes(ref, first)
            sums[0] = term if sums[0] is None else sums[0] + term
        for f, (a, b, group) in enumerate(fields):
            pot = two_potentials(y_parts[group], held, f, first, planes)
            for i, j in ((a, b),) if a == b else ((a, b), (b, a)):
                term = pot * psi[j]
                sums[i] = term if sums[i] is None else sums[i] + term
        for ref, total in zip(out_refs, sums):
            store_two(ref, first, total)


def sum_kernel(_, first_ref, second_ref, third_ref, out_ref):
    out_ref[...] = first_ref[...] + second_ref[...] + third_ref[...]


def permuted(value, axis, mask):
    count = lax.axis_size(axis)
    return lax.ppermute(value, axis, [(source, source ^ mask) for source in range(count)])


def exchanged(blocks, masks):
    return [
        permuted(block, "slab", mask) if mask else block for block, mask in zip(blocks, masks)
    ]


def paired_device(wavefunctions):
    _, planes, length, _ = wavefunctions.shape
    slabs = lax.axis_size("slab")
    table = jnp.asarray(cas_table(length))

    def call(body, shape, count, held, *operands):
        return pl.pallas_call(
            body,
            out_shape=[jax.ShapeDtypeStruct(shape, jnp.float32)] * count,
            scratch_shapes=[pltpu.VMEM(held, jnp.float32)] if held else [],
            compiler_params=pltpu.CompilerParams(vmem_limit_bytes=VMEM_LIMIT),
        )(table, *operands)

    own_pair = [(0, 0, 0)]
    cross_pairs = [(0, 1, 0), (0, 2, 1), (1, 2, 1)]
    own_rows, cross_rows = length // slabs, length // 2 // slabs
    own_held = (1, length * planes, length)
    cross_held = (3, length // 2 * planes, length)
    own_chips, cross_masks = own_masks(slabs)[::2], partner_masks(slabs)
    own_block = (1, 2 * own_rows, planes, length)
    cross_block = (3, cross_rows, planes, length)
    swap_block = (1, length // 2, planes, length)

    def forward(fields, block, count, held, *bands):
        body = functools.partial(forward_kernel, fields, slabs, len(bands))
        return call(body, block, count, held, *bands)

    def middle(fields, block, count, *blocks):
        body = functools.partial(middle_kernel, fields, slabs)
        return call(body, block, count, None, *blocks)

    def backward(fields, blocks, bands, terms, held):
        body = functools.partial(backward_kernel, fields, slabs, len(blocks), len(bands))
        shape = (planes, length, length)
        return call(body, shape, len(bands), held, *blocks, *bands, *terms)

    psi = wavefunctions[0]
    bands = [psi, permuted(psi, "band", 1), permuted(psi, "band", 2)]
    chips = exchanged(forward(own_pair, own_block, len(own_chips), own_held, psi), own_chips)
    cross_spec = forward(cross_pairs, cross_block, slabs, cross_held, *bands)
    cross_spec = exchanged(cross_spec, cross_masks)
    chips, cross_spec[0] = lax.optimization_barrier((chips, cross_spec[0]))
    swap = jnp.concatenate([chip[:, own_rows:] for chip in chips], axis=1)
    kept, swap = middle(own_pair, swap_block, 2, *chips, permuted(swap, "slab", 1))
    swap = permuted(swap, "slab", 1)
    chips = [
        jnp.concatenate([part[:, n * own_rows : (n + 1) * own_rows] for part in (kept, swap)], axis=1)
        for n in range(len(own_chips))
    ]
    cross_spec = middle(cross_pairs, cross_block, slabs, *cross_spec)
    cross_spec = exchanged(cross_spec, back_masks(slabs))
    chips, cross_spec = lax.optimization_barrier((chips, cross_spec))
    chips = exchanged(chips, own_chips)
    own_sum, to_x, to_y = backward(cross_pairs, cross_spec, bands, [], cross_held)
    (total,) = backward(own_pair, chips, [psi], [own_sum], own_held)
    sums = [total, permuted(to_x, "band", 1), permuted(to_y, "band", 2)]
    (total,) = call(sum_kernel, psi.shape, 1, None, *sums)
    return total[None]


def per_device(wavefunctions):
    length = wavefunctions.shape[2]
    columns, slabs = lax.axis_size("band"), lax.axis_size("slab")
    fits = (
        wavefunctions.shape[0] == 1
        and columns == 4
        and length == 128
        and wavefunctions.shape[1] % 8 == 0
        and slabs & (slabs - 1) == 0
        and slabs > 1
        and length % (4 * slabs) == 0
    )
    return paired_device(wavefunctions) if fits else general_device(wavefunctions)


def solution(mesh):
    in_specs = (P("band", "slab", None, None),)
    out_specs = P("band", "slab", None, None)
    return jax.shard_map(
        per_device, mesh=mesh, in_specs=in_specs, out_specs=out_specs, check_vma=False
    )
```

```python
import functools

import jax
import jax.numpy as jnp
import numpy as np
from jax import lax
from jax.experimental import pallas as pl
from jax.experimental.pallas import tpu as pltpu
from jax.sharding import PartitionSpec as P

HIGHEST_MODE = lax.Precision.HIGHEST
VMEM_LIMIT = 32 * 1024 * 1024


def cas_table(length):
    positions = np.arange(length)
    angles = 2.0 * np.pi / length * (positions[:, None] * positions[None, :] % length)
    return (np.cos(angles) + np.sin(angles)).astype(np.float32)


def squared_freqs(length):
    positions = np.arange(length)
    return (np.minimum(positions, length - positions) ** 2).astype(np.float32)


def coulomb(squared, length):
    kernel_scale = -0.25 * length**1.5 / 4.0 / float(length) ** 3
    return jnp.where(squared > 0, kernel_scale / jnp.maximum(squared, 1.0), 0.0)


def shifted(value, axis, steps):
    count = lax.axis_size(axis)
    pairs = [(source, (source + steps) % count) for source in range(count)]
    return lax.ppermute(value, axis, pairs)


def apply_table(form, field, table):
    return jnp.einsum(form, field, table, precision=HIGHEST_MODE)


def potentials(density):
    length = density.shape[2]
    table = jnp.asarray(cas_table(length))
    y_rows = length // lax.axis_size("slab")
    z_form = "pxyn,nk->pxyk"
    y_form = "pxnz,nk->pxkz"
    x_form = "pnyz,nk->pkyz"
    squared = jnp.asarray(squared_freqs(length))
    own_squared = lax.dynamic_slice_in_dim(squared, lax.axis_index("slab") * y_rows, y_rows)
    spec = apply_table(y_form, apply_table(z_form, density, table), table)
    spec = lax.all_to_all(spec, "slab", split_axis=2, concat_axis=1, tiled=True)
    spec = apply_table(x_form, spec, table) * coulomb(
        squared[:, None, None] + own_squared[None, :, None] + squared[None, None, :], length
    )
    spec = apply_table(x_form, spec, table)
    spec = lax.all_to_all(spec, "slab", split_axis=1, concat_axis=2, tiled=True)
    return apply_table(z_form, apply_table(y_form, spec, table), table)


def select_sum(selector, fields):
    return jnp.einsum("pb,pxyz->bxyz", selector, fields, precision=HIGHEST_MODE)


def general_device(wavefunctions):
    band_count = wavefunctions.shape[0]
    columns = lax.axis_size("band")
    half_loop = columns // 2
    left_index, right_index = np.triu_indices(band_count)
    left_select = (left_index[:, None] == np.arange(band_count)[None, :]).astype(np.float32)
    right_select = (
        (right_index[:, None] == np.arange(band_count)[None, :])
        & (left_index != right_index)[:, None]
    ).astype(np.float32)
    local_pots = potentials(wavefunctions[left_index] * wavefunctions[right_index])
    total_sum = select_sum(jnp.asarray(left_select), local_pots * wavefunctions[right_index])
    total_sum = total_sum + select_sum(
        jnp.asarray(right_select), local_pots * wavefunctions[left_index]
    )
    field_shape = wavefunctions.shape[1:]
    visitor = wavefunctions
    carried = jnp.zeros_like(wavefunctions)
    for shift_step in range(1, half_loop + 1):
        visitor, carried = shifted((visitor, carried), "band", 1)
        pair_density = (wavefunctions[:, None] * visitor[None, :]).reshape(
            (band_count * band_count,) + field_shape
        )
        pair_pots = potentials(pair_density).reshape((band_count, band_count) + field_shape)
        total_sum = total_sum + jnp.sum(pair_pots * visitor[None, :], axis=1)
        if shift_step < half_loop:
            contrib = jnp.sum(pair_pots * wavefunctions[:, None], axis=0)
        else:
            contrib = jnp.zeros_like(wavefunctions)
        carried = carried + contrib
    return total_sum + shifted(carried, "band", -half_loop)


def split_parts(value):
    high = value.astype(jnp.bfloat16)
    low = (value - high.astype(jnp.float32)).astype(jnp.bfloat16)
    return high, low


def product(left, right):
    return jnp.dot(left, right, preferred_element_type=jnp.float32)


def left_table(table):
    high, low = split_parts(table)
    if table.shape[1] <= 64:
        return jnp.concatenate([high, high, low], axis=1)
    return jnp.concatenate(
        [
            jnp.concatenate([high, high], axis=1),
            jnp.concatenate([low, jnp.zeros_like(low)], axis=1),
        ],
        axis=0,
    )


def left_apply(parts, value):
    high, low = split_parts(value)
    if value.shape[0] <= 64:
        return product(parts, jnp.concatenate([high, low, high], axis=0))
    both = product(parts, jnp.concatenate([high, low], axis=0))
    rows = parts.shape[0] // 2
    return both[:rows] + both[rows:]


def right_table(table):
    high, low = split_parts(table)
    return jnp.concatenate(
        [
            jnp.concatenate([high, low], axis=1),
            jnp.concatenate([high, jnp.zeros_like(low)], axis=1),
        ],
        axis=0,
    )


def right_apply(value, parts):
    both = product(jnp.concatenate(split_parts(value), axis=1), parts)
    columns = parts.shape[1] // 2
    return both[:, :columns] + both[:, columns:]


def two_planes(ref, first):
    return jnp.concatenate([ref[first], ref[first + 1]], axis=1)


def store_two(ref, first, value):
    length = ref.shape[2]
    ref[first] = value[:, :length]
    ref[first + 1] = value[:, length:]


def partner_masks(slabs):
    far = list(range(slabs - 1, slabs // 2 - 1, -1))
    near = list(range(1, slabs // 2)) + [0]
    return [mask for pair in zip(far, near) for mask in pair] if slabs > 1 else [0]


def back_masks(slabs):
    masks = partner_masks(slabs)
    for n in range(0, slabs - 2, 2):
        masks[n], masks[n + 1] = masks[n + 1], masks[n]
    return masks


def own_masks(slabs):
    chips = list(range(slabs - 2, -1, -2))
    middle = slabs // 2 // 2 - 1
    chips.insert(0, chips.pop(middle))
    return [chip + core for chip in chips for core in range(2)]


def masks_of(fields, slabs, back=False):
    if len(fields) == 1:
        return own_masks(slabs)
    return back_masks(slabs) if back else partner_masks(slabs)


def partner_rows(table_ref, masks, start, size):
    slab = lax.axis_index("slab")
    return jnp.concatenate(
        [
            table_ref[pl.ds(start + lax.bitwise_xor(slab, mask) * size, size), :]
            for mask in masks
        ],
        axis=0,
    )


def half_groups():
    column = lax.axis_index("band")
    return lax.rem(column, 2), lax.div(column, 2)


def group_starts(fields, length):
    if len(fields) == 1:
        return [0]
    return [group * (length // 2) for group in half_groups()]


def y_tables(fields, slabs, table_ref, back=False):
    starts = group_starts(fields, table_ref.shape[0])
    size = table_ref.shape[0] // slabs // (1 if len(fields) == 1 else 2)
    masks = masks_of(fields, slabs, back)
    return [partner_rows(table_ref, masks, start, size) for start in starts]


def forward_kernel(fields, slabs, bands, table_ref, *rest):
    psi_refs, out_refs, held = rest[:bands], rest[bands:-1], rest[-1]
    planes, length = psi_refs[0].shape[:2]
    per_slab = out_refs[0].shape[1]
    rows = held.shape[1] // planes
    y_parts = [left_table(table) for table in y_tables(fields, slabs, table_ref)]
    z_parts = right_table(table_ref[...])
    piece = per_slab * planes
    for first in range(0, planes, 2):
        psi = [two_planes(ref, first) for ref in psi_refs]
        for f, (a, b, group) in enumerate(fields):
            spec = left_apply(y_parts[group], psi[a] * psi[b])
            for side in range(2):
                held[f, pl.ds(first + side, rows, stride=planes), :] = spec[
                    :, side * length : (side + 1) * length
                ]
    for k, ref in enumerate(out_refs):
        for f in range(len(fields)):
            spec = right_apply(held[f, k * piece : (k + 1) * piece, :], z_parts)
            ref[f] = spec.reshape(per_slab, planes, length)


def folded_square(position, length):
    folded = jnp.minimum(position, length - position)
    return (folded * folded).astype(jnp.float32)


def middle_kernel(fields, slabs, table_ref, *rest):
    if len(fields) == 1:
        *chip_refs, swap_ref, kept_ref, swapped_ref = rest
        per_slab = chip_refs[0].shape[1] // 2
        in_refs, out_refs = [], []
        for n, ref in enumerate(chip_refs):
            half = pl.ds(n * per_slab, per_slab)
            in_refs += [ref.at[:, pl.ds(0, per_slab)], swap_ref.at[:, half]]
            out_refs += [kept_ref.at[:, half], swapped_ref.at[:, half]]
    else:
        in_refs, out_refs = rest[:slabs], rest[slabs:]
    _, per_slab, planes, length = in_refs[0].shape
    x_table, back_table = (
        partner_rows(table_ref, masks_of(fields, slabs, back), 0, planes)
        for back in (False, True)
    )
    x_parts, back_parts = left_table(x_table.T), left_table(back_table)
    in_plane = folded_square(
        lax.broadcasted_iota(jnp.int32, (length, length), 0), length
    ) + folded_square(lax.broadcasted_iota(jnp.int32, (length, length), 1), length)
    own_start = lax.axis_index("slab") * per_slab
    starts = [start + own_start for start in group_starts(fields, length)]
    for j in range(0, per_slab, 2):
        factors = [
            jnp.concatenate(
                [
                    coulomb(in_plane + folded_square(start + j + side, length), length)
                    for side in range(2)
                ],
                axis=1,
            )
            for start in starts
        ]
        for f, (_, _, group) in enumerate(fields):
            wide = jnp.concatenate(
                [
                    jnp.concatenate([ref[f, j + side] for ref in in_refs], axis=0)
                    for side in range(2)
                ],
                axis=1,
            )
            back = left_apply(back_parts, left_apply(x_parts, wide) * factors[group])
            for k, ref in enumerate(out_refs):
                for side in range(2):
                    ref[f, j + side] = back[
                        k * planes : (k + 1) * planes, side * length : (side + 1) * length
                    ]


def two_potentials(y_parts, held, f, first, planes):
    rows = held.shape[1] // planes
    spec = jnp.concatenate(
        [held[f, pl.ds(first + side, rows, stride=planes), :] for side in range(2)], axis=1
    )
    return left_apply(y_parts, spec)


def backward_kernel(fields, slabs, arrays, bands, table_ref, *rest):
    spec_refs, psi_refs = rest[:arrays], rest[arrays : arrays + bands]
    term_refs, out_refs, held = rest[arrays + bands : -bands - 1], rest[-bands - 1 : -1], rest[-1]
    _, per_slab, planes, length = spec_refs[0].shape
    z_parts = right_table(table_ref[...])
    y_parts = [left_table(table.T) for table in y_tables(fields, slabs, table_ref, True)]
    rows = per_slab * planes
    for k, ref in enumerate(spec_refs):
        for f in range(len(fields)):
            held[f, k * rows : (k + 1) * rows, :] = right_apply(
                ref[f].reshape(rows, length), z_parts
            )
    for first in range(0, planes, 2):
        psi = [two_planes(ref, first) for ref in psi_refs]
        sums = [None] * bands
        for ref in term_refs:
            term = two_planes(ref, first)
            sums[0] = term if sums[0] is None else sums[0] + term
        for f, (a, b, group) in enumerate(fields):
            pot = two_potentials(y_parts[group], held, f, first, planes)
            for i, j in ((a, b),) if a == b else ((a, b), (b, a)):
                term = pot * psi[j]
                sums[i] = term if sums[i] is None else sums[i] + term
        for ref, total in zip(out_refs, sums):
            store_two(ref, first, total)


def sum_kernel(_, first_ref, second_ref, third_ref, out_ref):
    out_ref[...] = first_ref[...] + second_ref[...] + third_ref[...]


def permuted(value, axis, mask):
    count = lax.axis_size(axis)
    return lax.ppermute(value, axis, [(source, source ^ mask) for source in range(count)])


def exchanged(blocks, masks):
    return [
        permuted(block, "slab", mask) if mask else block for block, mask in zip(blocks, masks)
    ]


def paired_device(wavefunctions):
    _, planes, length, _ = wavefunctions.shape
    slabs = lax.axis_size("slab")
    table = jnp.asarray(cas_table(length))

    def call(body, shape, count, held, *operands):
        return pl.pallas_call(
            body,
            out_shape=[jax.ShapeDtypeStruct(shape, jnp.float32)] * count,
            scratch_shapes=[pltpu.VMEM(held, jnp.float32)] if held else [],
            compiler_params=pltpu.CompilerParams(vmem_limit_bytes=VMEM_LIMIT),
        )(table, *operands)

    own_pair = [(0, 0, 0)]
    cross_pairs = [(0, 1, 0), (0, 2, 1), (1, 2, 1)]
    own_rows, cross_rows = length // slabs, length // 2 // slabs
    own_held = (1, length * planes, length)
    cross_held = (3, length // 2 * planes, length)
    own_chips, cross_masks = own_masks(slabs)[::2], partner_masks(slabs)
    own_block = (1, 2 * own_rows, planes, length)
    cross_block = (3, cross_rows, planes, length)
    swap_block = (1, length // 2, planes, length)

    def forward(fields, block, count, held, *bands):
        body = functools.partial(forward_kernel, fields, slabs, len(bands))
        return call(body, block, count, held, *bands)

    def middle(fields, block, count, *blocks):
        body = functools.partial(middle_kernel, fields, slabs)
        return call(body, block, count, None, *blocks)

    def backward(fields, blocks, bands, terms, held):
        body = functools.partial(backward_kernel, fields, slabs, len(blocks), len(bands))
        shape = (planes, length, length)
        return call(body, shape, len(bands), held, *blocks, *bands, *terms)

    psi = wavefunctions[0]
    bands = [psi, permuted(psi, "band", 1), permuted(psi, "band", 2)]
    chips = exchanged(forward(own_pair, own_block, len(own_chips), own_held, psi), own_chips)
    cross_spec = forward(cross_pairs, cross_block, slabs, cross_held, *bands)
    cross_spec = exchanged(cross_spec, cross_masks)
    chips, cross_spec[0] = lax.optimization_barrier((chips, cross_spec[0]))
    swap = jnp.concatenate([chip[:, own_rows:] for chip in chips], axis=1)
    kept, swap = middle(own_pair, swap_block, 2, *chips, permuted(swap, "slab", 1))
    swap = permuted(swap, "slab", 1)
    chips = [
        jnp.concatenate([part[:, n * own_rows : (n + 1) * own_rows] for part in (kept, swap)], axis=1)
        for n in range(len(own_chips))
    ]
    cross_spec = middle(cross_pairs, cross_block, slabs, *cross_spec)
    cross_spec = exchanged(cross_spec, back_masks(slabs))
    chips, cross_spec = lax.optimization_barrier((chips, cross_spec))
    chips = exchanged(chips, own_chips)
    own_sum, to_x, to_y = backward(cross_pairs, cross_spec, bands, [], cross_held)
    (total,) = backward(own_pair, chips, [psi], [own_sum], own_held)
    sums = [total, permuted(to_x, "band", 1), permuted(to_y, "band", 2)]
    (total,) = call(sum_kernel, psi.shape, 1, None, *sums)
    return total[None]


def per_device(wavefunctions):
    length = wavefunctions.shape[2]
    columns, slabs = lax.axis_size("band"), lax.axis_size("slab")
    fits = (
        wavefunctions.shape[0] == 1
        and columns == 4
        and length == 128
        and wavefunctions.shape[1] % 8 == 0
        and slabs & (slabs - 1) == 0
        and slabs > 1
        and length % (4 * slabs) == 0
    )
    return paired_device(wavefunctions) if fits else general_device(wavefunctions)


def solution(mesh):
    in_specs = (P("band", "slab", None, None),)
    out_specs = P("band", "slab", None, None)
    return jax.shard_map(
        per_device, mesh=mesh, in_specs=in_specs, out_specs=out_specs, check_vma=False
    )
```
